32 devices in a mesh: head: 2 (over core), blk: 16 (over z, y, x).
Axes of the slice: x: 2, y: 2, z: 4, core: 2. Of those that a mesh axis runs over, the one named last changes fastest.
Arguments:
- queries: bfloat16 [4096, 1024], P('blk', 'head'), may hold values from -5.5 to 5.5
- new_keys: bfloat16 [4096, 1024], P('blk', 'head'), may hold values from -5.5 to 5.5
- new_values: bfloat16 [4096, 1024], P('blk', 'head'), may hold values from -6 to 6
- sink_keys: bfloat16 [16, 4, 1024], P('blk', None, 'head'), may hold values from -16 to 16
- sink_values: bfloat16 [16, 4, 1024], P('blk', None, 'head'), may hold values from -6 to 6
- pool_keys: bfloat16 [16, 9, 512, 1024], P('blk', None, None, 'head'), may hold values from -6 to 6
- pool_values: bfloat16 [16, 9, 512, 1024], P('blk', None, None, 'head'), may hold values from -6 to 6
- block_ids: int32 [16, 9], replicated, may hold values from 1 to 64, as said below
- cache_lengths: int32 [16], replicated, may hold values from 4608 to 32768, as said below
- cross_keys: bfloat16 [16, 128, 1024], P('blk', None, 'head'), may hold values from -6 to 6
- cross_values: bfloat16 [16, 128, 1024], P('blk', None, 'head'), may hold values from -6 to 6
- enc_lengths: int32 [16], P('blk'), may hold values from 32 to 128
- hidden: bfloat16 [4096, 1024], P('blk', 'head'), may hold values from -6 to 6
- w_out_t: bfloat16 [1024, 1024], P(None, 'head'), may hold values from -0.1875 to 0.1875
- gain_self: float32 [1024], replicated, may hold values from 0.25 to 1.75
- bias_self: float32 [1024], replicated, may hold values from -0.5 to 0.5
- w_cross_q: bfloat16 [1024, 1024], P(None, 'head'), may hold values from -0.1875 to 0.1875
- w_cross_out_t: bfloat16 [1024, 1024], P(None, 'head'), may hold values from -0.1875 to 0.1875
- gain_cross: float32 [1024], replicated, may hold values from 0.25 to 1.75
- bias_cross: float32 [1024], replicated, may hold values from -0.5 to 0.5
Outputs:
- layer_out: bfloat16 [4096, 1024], P('blk', 'head')
The draws below stay inside these ranges and needn't reach their ends.
Inputs may be any that keep to these rules, and one draw needn't show every extreme that they name: `cache_lengths`: one request has exactly 32768 cached tokens and another exactly 4608. `block_ids`: entry [g, s] belongs to request (g - s - 1) mod 16; the 9 entries of request r hold the consecutive block numbers from (cache_lengths[r] - 4095) // 512 on, each once, in an order drawn from the seed.
All inputs are finite; a program needn't handle non-finite values.
Results may differ from the reference program's by a relative error of at most 0.02.
Values may be sent and summed in bfloat16 or wider, within the bound.
A program may use at most 192 MiB of HBM per device.

```python
import jax
import jax.numpy as jnp
from jax import lax

D = 1024
H = 16
HD = 64
BS = 512
WINDOW = 4096
SINK = 4
MAXLEN = 32768
SPAN = 256
ENC = 128
HH = 1024
SLOTS = 9
REQS = 16
TOKENS = 4096


def length_table(key):
    base_key = jax.random.fold_in(key, 101)
    first_key = jax.random.fold_in(base_key, 1)
    second_key = jax.random.fold_in(base_key, 2)
    third_key = jax.random.fold_in(base_key, 3)
    lowest = WINDOW + BS
    highest = MAXLEN
    drawn = jax.random.randint(first_key, (REQS,), lowest, highest + 1)
    top_slot = jax.random.randint(second_key, (), 0, REQS)
    low_slot = (top_slot + 1 + jax.random.randint(third_key, (), 0, REQS - 1)) % REQS
    index_row = jnp.arange(REQS)
    drawn = jnp.where(index_row == top_slot, highest, drawn)
    drawn = jnp.where(index_row == low_slot, lowest, drawn)
    return drawn.astype(jnp.int32)


def draw_cache_lengths(key, part):
    return length_table(key)


def draw_block_ids(key, part):
    lengths_all = length_table(key)
    order_keys = jax.random.split(jax.random.fold_in(key, 202), REQS)
    orders = jax.vmap(lambda one_key: jax.random.permutation(one_key, SLOTS))(order_keys)
    first_block = (lengths_all - WINDOW + 1) // BS
    holder_row = jnp.arange(REQS)[:, None]
    slot_col = jnp.arange(SLOTS)[None, :]
    request_of = (holder_row - slot_col - 1) % REQS
    return (first_block[request_of] + orders[request_of, slot_col]).astype(jnp.int32)


def drawn_pair(key):
    query_key = jax.random.fold_in(key, 11)
    other_key = jax.random.fold_in(key, 12)
    query_base = jnp.clip(jax.random.normal(query_key, (TOKENS, HH), jnp.float32), -5.5, 5.5)
    key_base = jnp.clip(jax.random.normal(other_key, (TOKENS, HH), jnp.float32), -5.5, 5.5)
    return (query_base, key_base)


def draw_queries(key, part):
    return drawn_pair(key)[0].astype(jnp.bfloat16)


def draw_new_keys(key, part):
    return drawn_pair(key)[1].astype(jnp.bfloat16)


def place_ends(values, own_key, smallest, high):
    spot = [jax.random.randint(jax.random.fold_in(own_key, axis), (), 0, length) for axis, length in enumerate(values.shape)]
    longest = values.shape.index(max(values.shape))
    neighbour = spot[:longest] + [(spot[longest] + 1) % values.shape[longest]] + spot[longest + 1:]
    return values.at[tuple(spot)].set(smallest).at[tuple(neighbour)].set(high)


def block_levels(stream_key, extent, cuts, least, largest):
    level, own = 1.0, jax.random.fold_in(stream_key, 6)
    for position, parts in cuts:
        steps = jnp.exp(jax.random.uniform(jax.random.fold_in(own, position), (parts,), jnp.float32, least / len(cuts), largest / len(cuts)))
        level = level * jnp.repeat(steps, extent[position] // parts).reshape([-1 if axis == position else 1 for axis in range(len(extent))])
    return level


def centred(key, shape, scale, limit, cuts=(), kind=jnp.bfloat16):
    values = scale * jax.random.normal(key, shape, jnp.float32)
    if cuts:
        values = values * block_levels(key, shape, cuts, -0.22, 0.18)
    return jnp.clip(values, -limit, limit).astype(kind)


def setup_inputs(seed: int = 0) -> dict:
    key_list = jax.random.split(jax.random.key(seed), 21)
    queries = draw_queries(jax.random.fold_in(key_list[20], 71), 0)
    new_keys = draw_new_keys(jax.random.fold_in(key_list[20], 71), 0)
    new_values = centred(key_list[2], (TOKENS, HH), 1.0, 6.0, ((0, 16), (1, 2)))
    sink_keys = centred(key_list[3], (REQS, SINK, HH), 3.0, 16.0, ((0, 16), (2, 2)))
    sink_values = centred(key_list[4], (REQS, SINK, HH), 1.0, 6.0, ((0, 16), (2, 2)))
    pool_keys = centred(key_list[5], (REQS, SLOTS, BS, HH), 1.0, 6.0, ((0, 16), (3, 2)))
    pool_values = centred(key_list[6], (REQS, SLOTS, BS, HH), 1.0, 6.0, ((0, 16), (3, 2)))
    block_ids = draw_block_ids(jax.random.fold_in(key_list[20], 71), 0)
    cache_lengths = draw_cache_lengths(jax.random.fold_in(key_list[20], 71), 0)
    cross_keys = centred(key_list[9], (REQS, ENC, HH), 1.0, 6.0, ((0, 16), (2, 2)))
    cross_values = centred(key_list[10], (REQS, ENC, HH), 1.0, 6.0, ((0, 16), (2, 2)))
    enc_lengths = place_ends(jax.random.randint(key_list[11], (REQS,), ENC // 4, ENC + 1), jax.random.fold_in(key_list[11], 1), ENC // 4, ENC).astype(jnp.int32)
    hidden = centred(key_list[12], (TOKENS, D), 1.0, 6.0, ((0, 16), (1, 2)))
    w_out_t = centred(key_list[13], (D, HH), HH ** -0.5, 0.1875, ((1, 2),))
    gain_self = jnp.clip(1.0 + 0.15 * jax.random.normal(key_list[14], (D,), jnp.float32), 0.25, 1.75)
    bias_self = jnp.clip(jax.random.uniform(key_list[15], (D,), jnp.float32, -0.5, 0.5), -0.5, 0.5)
    w_cross_q = centred(key_list[16], (D, HH), D ** -0.5, 0.1875, ((1, 2),))
    w_cross_out_t = centred(key_list[17], (D, HH), HH ** -0.5, 0.1875, ((1, 2),))
    gain_cross = jnp.clip(1.0 + 0.15 * jax.random.normal(key_list[18], (D,), jnp.float32), 0.25, 1.75)
    bias_cross = jnp.clip(jax.random.uniform(key_list[19], (D,), jnp.float32, -0.5, 0.5), -0.5, 0.5)
    return dict(queries=queries, new_keys=new_keys, new_values=new_values, sink_keys=sink_keys, sink_values=sink_values, pool_keys=pool_keys, pool_values=pool_values, block_ids=block_ids, cache_lengths=cache_lengths, cross_keys=cross_keys, cross_values=cross_values, enc_lengths=enc_lengths, hidden=hidden, w_out_t=w_out_t, gain_self=gain_self, bias_self=bias_self, w_cross_q=w_cross_q, w_cross_out_t=w_cross_out_t, gain_cross=gain_cross, bias_cross=bias_cross)


masked_score = -1e+30
norm_eps = 1e-05

def attend(query_rows, key_rows, value_rows, visible):
    row_count = query_rows.shape[0]
    key_count = key_rows.shape[0]
    query_heads = query_rows.astype(jnp.float32).reshape(row_count, H, HD)
    key_heads = key_rows.astype(jnp.float32).reshape(key_count, H, HD)
    value_heads = value_rows.astype(jnp.float32).reshape(key_count, H, HD)
    scores = jnp.einsum('qhd,khd->hqk', query_heads, key_heads) * HD ** (-0.5)
    scores = jnp.where(visible[None], scores, masked_score)
    row_top = lax.optimization_barrier(jnp.max(scores, axis=-1, keepdims=True))
    weights = jnp.where(visible[None], jnp.exp(scores - row_top), 0.0)
    row_total = lax.optimization_barrier(jnp.sum(weights, axis=-1))
    probabilities = lax.optimization_barrier(weights.astype(jnp.bfloat16)).astype(jnp.float32)
    summed = jnp.einsum('hqk,khd->qhd', probabilities, value_heads)
    result = summed / jnp.transpose(row_total)[:, :, None]
    return result.reshape(row_count, H * HD)

def layer_norm(pre_norm, gain_vec, bias_vec):
    row_mean = lax.optimization_barrier(jnp.mean(pre_norm, axis=-1, keepdims=True))
    centered = pre_norm - row_mean
    row_var = lax.optimization_barrier(jnp.mean(centered * centered, axis=-1, keepdims=True))
    return centered * lax.rsqrt(row_var + norm_eps) * gain_vec + bias_vec

def reference(queries, new_keys, new_values, sink_keys, sink_values, pool_keys, pool_values, block_ids, cache_lengths, cross_keys, cross_values, enc_lengths, hidden, w_out_t, gain_self, bias_self, w_cross_q, w_cross_out_t, gain_cross, bias_cross):

    def per_request(request):
        row_start = request * SPAN
        query_rows = lax.dynamic_slice_in_dim(queries, row_start, SPAN, 0)
        own_keys = lax.dynamic_slice_in_dim(new_keys, row_start, SPAN, 0)
        own_values = lax.dynamic_slice_in_dim(new_values, row_start, SPAN, 0)
        hidden_rows = lax.dynamic_slice_in_dim(hidden, row_start, SPAN, 0)
        cache_len = cache_lengths[request]
        slot_range = jnp.arange(SLOTS, dtype=jnp.int32)
        rows_held = ((request + 1 + slot_range) % REQS).astype(jnp.int32)
        block_keys = pool_keys[rows_held, slot_range].reshape(SLOTS * BS, H * HD)
        block_values = pool_values[rows_held, slot_range].reshape(SLOTS * BS, H * HD)
        held_ids = block_ids[rows_held, slot_range]
        positions = (held_ids[:, None] * BS + jnp.arange(BS, dtype=jnp.int32)[None, :]).reshape(-1)
        query_pos = cache_len + jnp.arange(SPAN, dtype=jnp.int32)
        window_vis = (positions[None, :] > query_pos[:, None] - WINDOW) & (positions[None, :] < cache_len)
        token_range = jnp.arange(SPAN, dtype=jnp.int32)
        own_vis = token_range[None, :] <= token_range[:, None]
        sink_vis = jnp.ones((SPAN, SINK), dtype=bool)
        all_keys = jnp.concatenate([sink_keys[request], block_keys, own_keys], axis=0)
        all_values = jnp.concatenate([sink_values[request], block_values, own_values], axis=0)
        all_vis = jnp.concatenate([sink_vis, window_vis, own_vis], axis=1)
        attended = attend(query_rows, all_keys, all_values, all_vis).astype(jnp.bfloat16)
        self_proj = jnp.dot(attended, w_out_t.T, preferred_element_type=jnp.float32)
        normed = layer_norm(hidden_rows.astype(jnp.float32) + self_proj, gain_self, bias_self).astype(jnp.bfloat16)
        cross_query = jnp.dot(normed, w_cross_q, preferred_element_type=jnp.float32).astype(jnp.bfloat16)
        enc_vis = jnp.broadcast_to(jnp.arange(ENC, dtype=jnp.int32)[None, :] < enc_lengths[request], (SPAN, ENC))
        context = attend(cross_query, cross_keys[request], cross_values[request], enc_vis).astype(jnp.bfloat16)
        cross_proj = jnp.dot(context, w_cross_out_t.T, preferred_element_type=jnp.float32)
        return layer_norm(normed.astype(jnp.float32) + cross_proj, gain_cross, bias_cross).astype(jnp.bfloat16)
    stacked = lax.map(per_request, jnp.arange(REQS, dtype=jnp.int32))
    return stacked.reshape(TOKENS, D)
```

```python
import functools

import jax
import jax.numpy as jnp
from jax import lax
from jax.experimental import pallas as pl
from jax.experimental.pallas import tpu as pltpu
from jax.sharding import PartitionSpec as P

HD = 64
WINDOW = 4096
GROUP = 4
LOG2E = 1.4426950408889634

masked_score = -1e30
norm_eps = 1e-05


def split_terms(stats):
    high = stats.astype(jnp.bfloat16).astype(jnp.float32)
    rest = stats - high
    middle = rest.astype(jnp.bfloat16).astype(jnp.float32)
    low = rest - middle
    return jnp.concatenate([high, middle, low, jnp.zeros_like(high)], axis=0).astype(jnp.bfloat16)


def attend_pairs(q_ref, k_ref, v_ref, bias, out_ref):
    rows, width = q_ref.shape
    lane = lax.broadcasted_iota(jnp.int32, (rows, 2 * HD), 1)
    first = lane < HD
    both = jnp.concatenate([bias, bias], axis=1)
    stats = []
    for pair in range(width // (2 * HD)):
        cols = slice(pair * 2 * HD, (pair + 1) * 2 * HD)
        q = q_ref[:, cols]
        zero = jnp.zeros_like(q)
        q2 = jnp.concatenate([jnp.where(first, q, zero), jnp.where(first, zero, q)], axis=0)
        scores = lax.dot_general(
            k_ref[:, cols], q2, (((1,), (1,)), ((), ())), preferred_element_type=jnp.float32
        )
        scores = scores * (HD ** (-0.5) * LOG2E) + both
        top = jnp.max(scores, axis=0, keepdims=True)
        weights = jnp.exp2(scores - top)
        total = jnp.sum(weights, axis=0, keepdims=True)
        summed = lax.dot_general(
            v_ref[:, cols],
            weights.astype(jnp.bfloat16),
            (((0,), (0,)), ((), ())),
            preferred_element_type=jnp.float32,
        )
        inverse = 1.0 / total
        lse = top + jnp.log2(total)
        base = pair * 2 * HD
        out_ref[base : base + HD, :] = (summed[:HD, :rows] * inverse[:, :rows]).astype(jnp.bfloat16)
        out_ref[base + HD : base + 2 * HD, :] = (
            summed[HD:, rows:] * inverse[:, rows:]
        ).astype(jnp.bfloat16)
        stats += [lse[:, :rows], lse[:, rows:]]
    out_ref[width : width + 4 * len(stats), :] = split_terms(jnp.concatenate(stats, axis=0))


def window_kernel(start_ref, q_ref, k_ref, v_ref, out_ref):
    keys, rows = k_ref.shape[0], q_ref.shape[0]
    relative = start_ref[0] + lax.broadcasted_iota(jnp.int32, (keys, rows), 0)
    token = lax.broadcasted_iota(jnp.int32, (keys, rows), 1)
    visible = (relative > token - WINDOW) & (relative < 0)
    attend_pairs(q_ref, k_ref, v_ref, jnp.where(visible, 0.0, masked_score), out_ref)


def local_kernel(sinks, q_ref, k_ref, v_ref, out_ref):
    keys, rows = k_ref.shape[0], q_ref.shape[0]
    index = lax.broadcasted_iota(jnp.int32, (keys, rows), 0)
    token = lax.broadcasted_iota(jnp.int32, (keys, rows), 1)
    visible = (index <= token) | ((index >= rows) & (index < rows + sinks))
    attend_pairs(q_ref, k_ref, v_ref, jnp.where(visible, 0.0, masked_score), out_ref)


def partial_call(kernel, prefix, q, k, v):
    rows, width = q.shape
    keys = k.shape[0]
    heads = width // HD
    whole = pl.BlockSpec(memory_space=pltpu.VMEM)
    smem = [pl.BlockSpec(memory_space=pltpu.SMEM)] * len(prefix)
    return pl.pallas_call(
        kernel,
        out_shape=jax.ShapeDtypeStruct((width + 4 * heads, rows), jnp.bfloat16),
        in_specs=smem + [whole] * 3,
        out_specs=whole,
        compiler_params=pltpu.CompilerParams(vmem_limit_bytes=32 * 1024 * 1024),
        cost_estimate=pl.CostEstimate(
            flops=4 * rows * keys * width, bytes_accessed=4 * keys * width, transcendentals=rows * keys * heads
        ),
    )(*prefix, q, k, v)


def unpack(part, width):
    heads = width // HD
    terms = part[width : width + 3 * heads].astype(jnp.float32)
    lse = terms[:heads] + terms[heads : 2 * heads] + terms[2 * heads :]
    return part[:width].reshape(heads, HD, -1).astype(jnp.float32), lse


def merge(parts, valid):
    lses = [jnp.where(ok, lse, masked_score) for (_, lse), ok in zip(parts, valid)]
    top = functools.reduce(jnp.maximum, lses)
    weights = [jnp.where(ok, jnp.exp2(lse - top), 0.0) for lse, ok in zip(lses, valid)]
    total = sum(weights)
    summed = sum(out * w[:, None, :] for (out, _), w in zip(parts, weights))
    total = jnp.where(total > 0.0, total, 1.0)
    return summed / total[:, None, :], top + jnp.log2(total)


def pack(merged):
    out, lse = merged
    return jnp.concatenate(
        [out.reshape(-1, out.shape[-1]).astype(jnp.bfloat16), split_terms(lse)], axis=0
    )


def moved(block, route):
    return lax.ppermute(block, "blk", route)


def head_whole(projected):
    return lax.psum(projected.astype(jnp.bfloat16), "head").astype(jnp.float32)


def full_norm(pre_norm, gain_vec, bias_vec):
    row_mean = jnp.mean(pre_norm, axis=-1, keepdims=True)
    centered = pre_norm - row_mean
    row_var = jnp.mean(centered * centered, axis=-1, keepdims=True)
    return centered * lax.rsqrt(row_var + norm_eps) * gain_vec + bias_vec


def cross_attend(cross_query, keys, values, enc_length):
    rows, width = cross_query.shape
    heads = width // HD
    q = cross_query.reshape(rows, heads, HD)
    k = keys.reshape(-1, heads, HD)
    v = values.reshape(-1, heads, HD)
    scores = jnp.einsum("qhd,khd->hqk", q, k, preferred_element_type=jnp.float32) * HD ** (-0.5)
    visible = (jnp.arange(k.shape[0], dtype=jnp.int32) < enc_length)[None, None, :]
    scores = jnp.where(visible, scores, masked_score)
    top = jnp.max(scores, axis=-1, keepdims=True)
    weights = jnp.where(visible, jnp.exp(scores - top), 0.0)
    total = jnp.sum(weights, axis=-1)
    summed = jnp.einsum(
        "hqk,khd->hqd", weights.astype(jnp.bfloat16), v, preferred_element_type=jnp.float32
    )
    result = summed / total[..., None]
    return jnp.transpose(result, (1, 0, 2)).reshape(rows, width).astype(jnp.bfloat16)


def per_device(
    queries,
    new_keys,
    new_values,
    sink_keys,
    sink_values,
    pool_keys,
    pool_values,
    block_ids,
    cache_lengths,
    cross_keys,
    cross_values,
    enc_lengths,
    hidden,
    w_out_t,
    gain_self,
    bias_self,
    w_cross_q,
    w_cross_out_t,
    gain_cross,
    bias_cross,
):
    device = lax.axis_index("blk")
    count = lax.axis_size("blk")
    lane = device % GROUP
    rows, width = queries.shape
    slots, block_rows = pool_keys.shape[1:3]
    sinks = sink_keys.shape[1]

    def across(block, distance, only_last=False):
        route = [
            (i, (i + GROUP * distance) % count)
            for i in range(count)
            if not only_last or i % GROUP == GROUP - 1
        ]
        return moved(block, route)

    def inside(block, shift):
        route = [(i, i - i % GROUP + (i + shift) % GROUP) for i in range(count)]
        return moved(block, route)

    stack = [queries, across(queries, 1), across(queries, 2), across(queries, 3, True)]
    partials = {}
    for s in range(1, slots + 1):
        step, shift = divmod(s, GROUP)
        if shift:
            content = jnp.where(lane + shift >= GROUP, stack[step + 1], stack[step])
            query_rows = inside(content, shift)
        else:
            query_rows = stack[step]
        asker = (device - s) % count
        start = block_ids[device, s - 1] * block_rows - cache_lengths[asker]
        part = partial_call(
            window_kernel, [start.reshape(1)], query_rows, pool_keys[0, s - 1], pool_values[0, s - 1]
        )
        partials[s] = unpack(inside(part, -shift) if shift else part, width)

    padding = jnp.zeros((128 - sinks, width), jnp.bfloat16)
    own = partial_call(
        functools.partial(local_kernel, sinks),
        [],
        queries,
        jnp.concatenate([new_keys, sink_keys[0], padding], axis=0),
        jnp.concatenate([new_values, sink_values[0], padding], axis=0),
    )
    back = {}
    for distance in (1, 2, 3):
        members = [s for s in partials if distance * GROUP - (GROUP - 1) <= s < (distance + 1) * GROUP]
        flags = [(lane + s) // GROUP == distance for s in members]
        group_part = pack(merge([partials[s] for s in members], flags))
        back[distance] = unpack(across(group_part, -distance, distance == 3), width)
    near = [s for s in partials if s < GROUP]
    flags = [(lane + s) // GROUP == 0 for s in near] + [True, True, True, lane == GROUP - 1]
    merged, _ = merge(
        [partials[s] for s in near] + [unpack(own, width), back[1], back[2], back[3]], flags
    )
    attended_t = merged.reshape(width, rows).astype(jnp.bfloat16)

    self_proj = lax.dot_general(
        attended_t, w_out_t, (((0,), (1,)), ((), ())), preferred_element_type=jnp.float32
    )
    head_index = lax.axis_index("head")
    col_start = head_index * width
    own_cols = lax.dynamic_slice_in_dim(self_proj, col_start, width, 1) + hidden.astype(jnp.float32)
    pre_full = head_whole(lax.dynamic_update_slice_in_dim(self_proj, own_cols, col_start, 1))
    normed_full = full_norm(pre_full, gain_self, bias_self).astype(jnp.bfloat16)
    cross_query = jnp.dot(normed_full, w_cross_q, preferred_element_type=jnp.float32).astype(
        jnp.bfloat16
    )
    context = cross_attend(cross_query, cross_keys[0], cross_values[0], enc_lengths[0])
    cross_proj = lax.dot_general(
        context, w_cross_out_t, (((1,), (1,)), ((), ())), preferred_element_type=jnp.float32
    )
    own_normed = lax.dynamic_slice_in_dim(normed_full, col_start, width, 1).astype(jnp.float32)
    own_cross = lax.dynamic_slice_in_dim(cross_proj, col_start, width, 1) + own_normed
    second_full = head_whole(lax.dynamic_update_slice_in_dim(cross_proj, own_cross, col_start, 1))
    full_out = full_norm(second_full, gain_cross, bias_cross).astype(jnp.bfloat16)
    return lax.dynamic_slice_in_dim(full_out, col_start, width, 1)


def solution(mesh):
    placed = (
        P("blk", "head"),
        P("blk", "head"),
        P("blk", "head"),
        P("blk", None, "head"),
        P("blk", None, "head"),
        P("blk", None, None, "head"),
        P("blk", None, None, "head"),
        P(),
        P(),
        P("blk", None, "head"),
        P("blk", None, "head"),
        P("blk"),
        P("blk", "head"),
        P(None, "head"),
        P(),
        P(),
        P(None, "head"),
        P(None, "head"),
        P(),
        P(),
    )
    return jax.shard_map(
        per_device, mesh=mesh, in_specs=placed, out_specs=P("blk", "head"), check_vma=False
    )
```

```python
import functools

import jax
import jax.numpy as jnp
from jax import lax
from jax.experimental import pallas as pl
from jax.experimental.pallas import tpu as pltpu
from jax.sharding import PartitionSpec as P

HD = 64
WINDOW = 4096
GROUP = 4
LOG2E = 1.4426950408889634

masked_score = -1e30
norm_eps = 1e-05


def split_terms(stats):
    high = stats.astype(jnp.bfloat16).astype(jnp.float32)
    rest = stats - high
    middle = rest.astype(jnp.bfloat16).astype(jnp.float32)
    low = rest - middle
    return jnp.concatenate([high, middle, low, jnp.zeros_like(high)], axis=0).astype(jnp.bfloat16)


def attend_pairs(q, k_ref, v_ref, bias):
    rows, width = q.shape
    lane = lax.broadcasted_iota(jnp.int32, (rows, 2 * HD), 1)
    first = lane < HD
    both = jnp.concatenate([bias, bias], axis=1)
    outs, stats = [], []
    for pair in range(width // (2 * HD)):
        cols = slice(pair * 2 * HD, (pair + 1) * 2 * HD)
        part = q[:, cols]
        zero = jnp.zeros_like(part)
        q2 = jnp.concatenate([jnp.where(first, part, zero), jnp.where(first, zero, part)], axis=0)
        scores = lax.dot_general(
            k_ref[:, cols], q2, (((1,), (1,)), ((), ())), preferred_element_type=jnp.float32
        )
        scores = scores * (HD ** (-0.5) * LOG2E) + both
        top = jnp.max(scores, axis=0, keepdims=True)
        weights = jnp.exp2(scores - top)
        total = jnp.sum(weights, axis=0, keepdims=True)
        summed = lax.dot_general(
            v_ref[:, cols],
            weights.astype(jnp.bfloat16),
            (((0,), (0,)), ((), ())),
            preferred_element_type=jnp.float32,
        )
        inverse = 1.0 / total
        lse = top + jnp.log2(total)
        outs += [summed[:HD, :rows] * inverse[:, :rows], summed[HD:, rows:] * inverse[:, rows:]]
        stats += [lse[:, :rows], lse[:, rows:]]
    return outs, stats


def store_part(out_ref, outs, stats):
    for i, out in enumerate(outs):
        out_ref[i * HD : (i + 1) * HD, :] = out.astype(jnp.bfloat16)
    width = len(outs) * HD
    out_ref[width : width + 4 * len(outs), :] = split_terms(jnp.concatenate(stats, axis=0))


def merge(refs, flags):
    heads = refs[0].shape[0] // (HD + 4)
    width = heads * HD
    lses = []
    for ref, flag in zip(refs, flags):
        terms = ref[width:, :].astype(jnp.float32)
        lse = terms[:heads] + terms[heads : 2 * heads] + terms[2 * heads : 3 * heads]
        lses.append(lse if flag is True else jnp.where(flag, lse, 2.0 * masked_score))
    top = functools.reduce(jnp.maximum, lses)
    weights = [jnp.exp2(lse - top) for lse in lses]
    total = sum(weights)
    inverse = 1.0 / total
    weights = [w * inverse for w in weights]
    lse = top + jnp.log2(total)
    outs, stats = [], []
    for head in range(heads):
        rows = slice(head * HD, (head + 1) * HD)
        outs.append(
            sum(ref[rows, :].astype(jnp.float32) * w[head : head + 1] for ref, w in zip(refs, weights))
        )
        stats.append(lse[head : head + 1])
    return outs, stats


def layer_kernel(
    count,
    slots,
    sinks,
    block_ids,
    cache_lengths,
    enc_lengths,
    queries,
    new_keys,
    new_values,
    sink_keys,
    sink_values,
    pool_keys,
    pool_values,
    cross_keys,
    cross_values,
    hidden,
    w_out,
    gain_self,
    bias_self,
    w_query,
    w_cross,
    gain_cross,
    bias_cross,
    out,
    k_buf,
    v_buf,
    k_own,
    v_own,
    q_far,
    q_near,
    part,
    near,
    merged,
    far,
    own_part,
    own_merged,
    w_mine,
    w_theirs,
    w_theirs_query,
    cross_mine,
    cross_theirs,
    hidden_theirs,
    turned,
    turned_theirs,
    out_send,
    out_theirs,
    kv_sem,
    own_sem,
    qf_send,
    qf_recv,
    qn_send,
    qn_recv,
    pn_send,
    pn_recv,
    pf_send,
    pf_recv,
    sib_send,
    sib_recv,
):
    device = lax.axis_index("blk")
    head = lax.axis_index("head")
    lane = lax.rem(device, GROUP)
    base = device - lane
    rows, width = queries.shape
    half = rows // 2
    mesh_id = pl.DeviceIdType.MESH

    def at_far(distance):
        return (head, lax.rem(device + count + GROUP * distance, count))

    def at_near(shift):
        return (head, base + lax.rem(lane + GROUP + shift, GROUP))

    sibling = (1 - head, device)

    local = [
        pltpu.make_async_copy(w_out, w_mine.at[0], own_sem.at[0]),
        pltpu.make_async_copy(w_cross, w_mine.at[1], own_sem.at[1]),
        pltpu.make_async_copy(cross_keys.at[0], cross_mine.at[0], own_sem.at[2]),
        pltpu.make_async_copy(cross_values.at[0], cross_mine.at[1], own_sem.at[3]),
    ]
    order = [4, 1, 2, 3, 5, 6, 7, 8, 9]

    def pool_copies(s):
        return (
            pltpu.make_async_copy(pool_keys.at[0, s - 1], k_buf.at[s - 1], kv_sem.at[0, s - 1]),
            pltpu.make_async_copy(pool_values.at[0, s - 1], v_buf.at[s - 1], kv_sem.at[1, s - 1]),
        )

    for s in order:
        for copy in pool_copies(s):
            copy.start()
    for copy in local:
        copy.start()

    barrier = pltpu.get_barrier_semaphore()
    partners = [at_far(d) for d in (1, 2, 3, -1, -2, -3)] + [at_near(d) for d in (1, 2, 3)] + [sibling]
    for partner in partners:
        pl.semaphore_signal(barrier, inc=1, device_id=partner, device_id_type=mesh_id)

    k_own[:rows, :] = new_keys[...]
    v_own[:rows, :] = new_values[...]
    k_own[rows : rows + 16, :] = sink_keys[...]
    v_own[rows : rows + 16, :] = sink_values[...]
    pad = k_own.shape[0] - rows - 16
    k_own[rows + 16 :, :] = jnp.zeros((pad, width), jnp.bfloat16)
    v_own[rows + 16 :, :] = jnp.zeros((pad, width), jnp.bfloat16)

    pl.semaphore_wait(barrier, len(partners))

    def remote(source, target, send, recv, device_id):
        return pltpu.make_async_remote_copy(
            src_ref=source,
            dst_ref=target,
            send_sem=send,
            recv_sem=recv,
            device_id=device_id,
            device_id_type=mesh_id,
        )

    def query_far(distance):
        i = distance - 1
        return remote(queries, q_far.at[i], qf_send.at[i], qf_recv.at[i], at_far(distance))

    def query_near(s, source):
        return remote(source, q_near.at[s - 1], qn_send.at[s - 1], qn_recv.at[s - 1], at_near(s % GROUP))

    def part_near(s):
        shift = lax.rem(s, GROUP)
        target = (head, base + lax.rem(lane + GROUP - shift, GROUP))
        return remote(part.at[s - 1], near.at[s - 1], pn_send.at[s - 1], pn_recv.at[s - 1], target)

    def part_far(distance, source):
        i = distance - 1
        return remote(source, far.at[i], pf_send.at[i], pf_recv.at[i], at_far(-distance))

    query_far(2).start()
    query_far(1).start()
    last = lane == GROUP - 1

    @pl.when(last)
    def _():
        query_far(3).start()

    @pl.when(jnp.logical_not(last))
    def _():
        far[2] = jnp.zeros(far.shape[1:], far.dtype)

    moves = [s for s in range(1, slots + 1) if s % GROUP]

    def forward(distance):
        source = queries if distance == 0 else q_far.at[distance - 1]
        for s in moves:
            if s // GROUP == distance or s // GROUP + 1 == distance:
                wraps = lane + s % GROUP >= GROUP
                here = wraps if s // GROUP + 1 == distance else jnp.logical_not(wraps)

                @pl.when(here)
                def _():
                    query_near(s, source).start()

    forward(0)
    other_rows = pl.ds(pl.multiple_of((1 - head) * half, half), half)
    to_sibling = [
        (hidden.at[other_rows, :], hidden_theirs),
        (w_out, w_theirs.at[0]),
        (cross_keys.at[0], cross_theirs.at[0]),
        (cross_values.at[0], cross_theirs.at[1]),
        (w_query, w_theirs_query),
        (w_cross, w_theirs.at[1]),
    ]
    shared = [
        remote(a, b, sib_send.at[i], sib_recv.at[i], sibling) for i, (a, b) in enumerate(to_sibling)
    ]
    for copy in shared:
        copy.start()

    index = lax.broadcasted_iota(jnp.int32, (k_own.shape[0], rows), 0)
    token = lax.broadcasted_iota(jnp.int32, (k_own.shape[0], rows), 1)
    visible = (index <= token) | ((index >= rows) & (index < rows + sinks))
    bias = jnp.where(visible, 0.0, masked_score)
    store_part(own_part, *attend_pairs(queries[...], k_own, v_own, bias))

    def compute(s, q_ref, target):
        for copy in pool_copies(s):
            copy.wait()
        asker = lax.rem(device + count - s, count)
        keys = k_buf.shape[1]
        start = block_ids[device, s - 1] * keys - cache_lengths[asker]
        relative = start + lax.broadcasted_iota(jnp.int32, (keys, rows), 0)
        token = lax.broadcasted_iota(jnp.int32, (keys, rows), 1)
        visible = (relative > token - WINDOW) & (relative < 0)
        bias = jnp.where(visible, 0.0, masked_score)
        store_part(target, *attend_pairs(q_ref[...], k_buf.at[s - 1], v_buf.at[s - 1], bias))

    def moved_step(s, carry=0):
        remote(
            queries, q_near.at[s - 1], qn_send.at[s - 1], qn_recv.at[s - 1], sibling
        ).wait_recv()
        compute(s, q_near.at[s - 1], part.at[s - 1])
        part_near(s).start()
        return carry

    def wait_near(s, condition):
        @pl.when(condition)
        def _():
            part_near(s).wait_recv()

    query_far(1).wait_recv()
    forward(1)
    compute(4, q_far.at[0], near.at[3])
    query_far(2).wait_recv()
    forward(2)
    lax.fori_loop(1, 4, moved_step, 0)

    @pl.when(last)
    def _():
        query_far(3).wait_recv()

    forward(3)
    lax.fori_loop(5, 8, moved_step, 0)
    compute(8, q_far.at[1], near.at[7])

    def merge_group(distance):
        refs, flags = [], []
        for j in range(GROUP):
            s = GROUP * distance - lane + j
            inside = s <= slots
            wait_near(s, jnp.logical_and(inside, lane != j))
            refs.append(near.at[jnp.minimum(s, slots) - 1])
            flags.append(True if distance == 1 else inside)
        store_part(merged.at[distance - 1], *merge(refs, flags))
        part_far(distance, merged.at[distance - 1]).start()

    moved_step(9)
    merge_group(1)
    merge_group(2)

    @pl.when(last)
    def _():
        part_near(9).wait_recv()
        part_far(3, near.at[8]).start()

    refs, flags = [own_part], [True]
    for s in range(1, GROUP):
        inside = lane + s < GROUP
        wait_near(s, inside)
        refs.append(near.at[s - 1])
        flags.append(inside)
    store_part(own_merged, *merge(refs, flags))
    part_far(1, merged.at[0]).wait_recv()
    part_far(2, merged.at[1]).wait_recv()

    @pl.when(last)
    def _():
        part_far(3, near.at[8]).wait_recv()

    outs, _ = merge([own_merged] + [far.at[i] for i in range(3)], [True, True, True, last])

    for i in range(2):
        cut = slice(i * half, (i + 1) * half)
        turned[i] = jnp.concatenate([o[:, cut] for o in outs], axis=0).T.astype(jnp.bfloat16)
    send_turned = remote(turned.at[1 - head], turned_theirs, sib_send.at[6], sib_recv.at[6], sibling)
    send_turned.start()

    for copy in local:
        copy.wait()
    for copy in shared:
        copy.wait()

    def project_back(rows_in, weight):
        return lax.dot_general(
            rows_in, weight, (((1,), (1,)), ((), ())), preferred_element_type=jnp.float32
        )

    def ordered(mine, theirs):
        is_first = head == 0
        return jnp.concatenate(
            [jnp.where(is_first, mine, theirs), jnp.where(is_first, theirs, mine)], axis=1
        )

    def full_norm(pre_norm, gain, bias_row):
        row_mean = jnp.mean(pre_norm, axis=-1, keepdims=True)
        centered = pre_norm - row_mean
        row_var = jnp.mean(centered * centered, axis=-1, keepdims=True)
        return centered * lax.rsqrt(row_var + norm_eps) * gain[...] + bias_row[...]

    own_rows = pl.ds(pl.multiple_of(head * half, half), half)
    residual = ordered(
        hidden[own_rows, :].astype(jnp.float32), hidden_theirs[...].astype(jnp.float32)
    )
    pre = residual + project_back(turned[head], w_mine[0])
    send_turned.wait()
    pre = pre + project_back(turned_theirs[...], w_theirs[0])
    normed = full_norm(pre, gain_self, bias_self).astype(jnp.bfloat16)

    enc = cross_mine.shape[1]
    seen = lax.broadcasted_iota(jnp.int32, (enc, half), 0) < enc_lengths[0]
    enc_bias = jnp.where(seen, 0.0, masked_score)
    second = normed.astype(jnp.float32)
    for wq, kv, w_back in (
        (w_query, cross_mine, w_mine.at[1]),
        (w_theirs_query, cross_theirs, w_theirs.at[1]),
    ):
        cross_query = jnp.dot(normed, wq[...], preferred_element_type=jnp.float32).astype(jnp.bfloat16)
        context, _ = attend_pairs(cross_query, kv.at[0], kv.at[1], enc_bias)
        context = jnp.concatenate(context, axis=0).T.astype(jnp.bfloat16)
        second = second + project_back(context, w_back[...])
    result = full_norm(second, gain_cross, bias_cross)
    left, right = result[:, :width], result[:, width:]
    is_first = head == 0
    out_send[...] = jnp.where(is_first, right, left).astype(jnp.bfloat16)
    send_out = remote(out_send, out_theirs, sib_send.at[7], sib_recv.at[7], sibling)
    send_out.start()
    out[own_rows, :] = jnp.where(is_first, left, right).astype(jnp.bfloat16)

    for s in moves:
        query_near(s, queries).wait_send()
        part_near(s).wait_send()
    for distance in (1, 2):
        query_far(distance).wait_send()
        part_far(distance, merged.at[distance - 1]).wait_send()

    @pl.when(last)
    def _():
        query_far(3).wait_send()
        part_far(3, near.at[8]).wait_send()

    send_out.wait()
    out[other_rows, :] = out_theirs[...]


def per_device(
    queries,
    new_keys,
    new_values,
    sink_keys,
    sink_values,
    pool_keys,
    pool_values,
    block_ids,
    cache_lengths,
    cross_keys,
    cross_values,
    enc_lengths,
    hidden,
    w_out_t,
    gain_self,
    bias_self,
    w_cross_q,
    w_cross_out_t,
    gain_cross,
    bias_cross,
):
    count = lax.axis_size("blk")
    rows, width = queries.shape
    slots, keys = pool_keys.shape[1:3]
    sinks = sink_keys.shape[1]
    enc = cross_keys.shape[1]
    full = w_out_t.shape[0]
    half = rows // 2
    packed = width + 4 * (width // HD)
    pad = ((0, 16 - sinks), (0, 0))
    whole = pl.BlockSpec(memory_space=pltpu.VMEM)
    smem = pl.BlockSpec(memory_space=pltpu.SMEM)
    hbm = pl.BlockSpec(memory_space=pl.ANY)

    def buf(*shape):
        return pltpu.VMEM(shape, jnp.bfloat16)

    dma = pltpu.SemaphoreType.DMA
    return pl.pallas_call(
        functools.partial(layer_kernel, count, slots, sinks),
        out_shape=jax.ShapeDtypeStruct((rows, width), jnp.bfloat16),
        in_specs=[smem] * 3
        + [whole] * 5
        + [hbm] * 4
        + [whole, hbm, whole, whole, whole, hbm, whole, whole],
        out_specs=whole,
        scratch_shapes=[
            buf(slots, keys, width),
            buf(slots, keys, width),
            buf(rows + 128, width),
            buf(rows + 128, width),
            buf(3, rows, width),
            buf(slots, rows, width),
            buf(slots, packed, rows),
            buf(slots, packed, rows),
            buf(2, packed, rows),
            buf(3, packed, rows),
            buf(packed, rows),
            buf(packed, rows),
            buf(2, full, width),
            buf(2, full, width),
            buf(full, width),
            buf(2, enc, width),
            buf(2, enc, width),
            buf(half, width),
            buf(2, half, width),
            buf(half, width),
            buf(half, width),
            buf(half, width),
            dma((2, slots)),
            dma((4,)),
            dma((3,)),
            dma((3,)),
            dma((slots,)),
            dma((slots,)),
            dma((slots,)),
            dma((slots,)),
            dma((3,)),
            dma((3,)),
            dma((8,)),
            dma((8,)),
        ],
        compiler_params=pltpu.CompilerParams(
            collective_id=0, has_side_effects=True, vmem_limit_bytes=52 * 1024 * 1024
        ),
        cost_estimate=pl.CostEstimate(
            flops=4 * rows * keys * width * slots,
            bytes_accessed=4 * keys * width * slots,
            transcendentals=rows * keys * slots * (width // HD),
        ),
    )(
        block_ids,
        cache_lengths,
        enc_lengths,
        queries,
        new_keys,
        new_values,
        jnp.pad(sink_keys[0], pad),
        jnp.pad(sink_values[0], pad),
        pool_keys,
        pool_values,
        cross_keys,
        cross_values,
        hidden,
        w_out_t,
        gain_self.reshape(1, -1),
        bias_self.reshape(1, -1),
        w_cross_q,
        w_cross_out_t,
        gain_cross.reshape(1, -1),
        bias_cross.reshape(1, -1),
    )


def solution(mesh):
    placed = (
        P("blk", "head"),
        P("blk", "head"),
        P("blk", "head"),
        P("blk", None, "head"),
        P("blk", None, "head"),
        P("blk", None, None, "head"),
        P("blk", None, None, "head"),
        P(),
        P(),
        P("blk", None, "head"),
        P("blk", None, "head"),
        P("blk"),
        P("blk", "head"),
        P(None, "head"),
        P(),
        P(),
        P(None, "head"),
        P(None, "head"),
        P(),
        P(),
    )
    return jax.shard_map(
        per_device, mesh=mesh, in_specs=placed, out_specs=P("blk", "head"), check_vma=False
    )
```

```python
import functools

import jax
import jax.numpy as jnp
from jax import lax
from jax.experimental import pallas as pl
from jax.experimental.pallas import tpu as pltpu
from jax.sharding import PartitionSpec as P

HD = 64
WINDOW = 4096
GROUP = 4
LOG2E = 1.4426950408889634

masked_score = -1e30
norm_eps = 1e-05


def split_terms(stats):
    high = stats.astype(jnp.bfloat16).astype(jnp.float32)
    rest = stats - high
    middle = rest.astype(jnp.bfloat16).astype(jnp.float32)
    low = rest - middle
    return jnp.concatenate([high, middle, low, jnp.zeros_like(high)], axis=0).astype(jnp.bfloat16)


def attend_pairs(q, k_ref, v_ref, bias):
    rows, width = q.shape
    lane = lax.broadcasted_iota(jnp.int32, (rows, 2 * HD), 1)
    first = lane < HD
    both = jnp.concatenate([bias, bias], axis=1)
    outs, stats = [], []
    for pair in range(width // (2 * HD)):
        cols = slice(pair * 2 * HD, (pair + 1) * 2 * HD)
        part = q[:, cols]
        zero = jnp.zeros_like(part)
        q2 = jnp.concatenate([jnp.where(first, part, zero), jnp.where(first, zero, part)], axis=0)
        scores = lax.dot_general(
            k_ref[:, cols], q2, (((1,), (1,)), ((), ())), preferred_element_type=jnp.float32
        )
        scores = scores * (HD ** (-0.5) * LOG2E) + both
        top = jnp.max(scores, axis=0, keepdims=True)
        weights = jnp.exp2(scores - top)
        total = jnp.sum(weights, axis=0, keepdims=True)
        summed = lax.dot_general(
            v_ref[:, cols],
            weights.astype(jnp.bfloat16),
            (((0,), (0,)), ((), ())),
            preferred_element_type=jnp.float32,
        )
        inverse = 1.0 / total
        lse = top + jnp.log2(total)
        outs += [summed[:HD, :rows] * inverse[:, :rows], summed[HD:, rows:] * inverse[:, rows:]]
        stats += [lse[:, :rows], lse[:, rows:]]
    return outs, stats


def store_part(out_ref, outs, stats):
    for i, out in enumerate(outs):
        out_ref[i * HD : (i + 1) * HD, :] = out.astype(jnp.bfloat16)
    width = len(outs) * HD
    out_ref[width : width + 4 * len(outs), :] = split_terms(jnp.concatenate(stats, axis=0))


def merge(refs, flags):
    heads = refs[0].shape[0] // (HD + 4)
    width = heads * HD
    lses = []
    for ref, flag in zip(refs, flags):
        terms = ref[width:, :].astype(jnp.float32)
        lse = terms[:heads] + terms[heads : 2 * heads] + terms[2 * heads : 3 * heads]
        lses.append(lse if flag is True else jnp.where(flag, lse, 2.0 * masked_score))
    top = functools.reduce(jnp.maximum, lses)
    weights = [jnp.exp2(lse - top) for lse in lses]
    total = sum(weights)
    inverse = 1.0 / total
    weights = [w * inverse for w in weights]
    lse = top + jnp.log2(total)
    outs, stats = [], []
    for head in range(heads):
        rows = slice(head * HD, (head + 1) * HD)
        outs.append(
            sum(ref[rows, :].astype(jnp.float32) * w[head : head + 1] for ref, w in zip(refs, weights))
        )
        stats.append(lse[head : head + 1])
    return outs, stats


def layer_kernel(
    count,
    slots,
    sinks,
    block_ids,
    cache_lengths,
    enc_lengths,
    queries,
    new_keys,
    new_values,
    sink_pair,
    pool_keys,
    pool_values,
    cross_keys,
    cross_values,
    hidden,
    w_out,
    gain_self,
    bias_self,
    w_query,
    w_cross,
    gain_cross,
    bias_cross,
    out,
    k_buf,
    v_buf,
    k_own,
    v_own,
    q_own,
    hidden_mine,
    w_query_mine,
    norms,
    q_far,
    q_near,
    part,
    near,
    merged,
    far,
    own_part,
    own_merged,
    w_mine,
    w_theirs,
    w_theirs_query,
    cross_mine,
    cross_theirs,
    hidden_theirs,
    turned,
    turned_theirs,
    out_send,
    out_theirs,
    kv_sem,
    own_sem,
    qf_send,
    qf_recv,
    qn_send,
    qn_recv,
    pn_send,
    pn_recv,
    pf_send,
    pf_recv,
    sib_send,
    sib_recv,
):
    device = lax.axis_index("blk")
    head = lax.axis_index("head")
    lane = lax.rem(device, GROUP)
    base = device - lane
    rows, width = queries.shape
    half = rows // 2
    mesh_id = pl.DeviceIdType.MESH

    def at_far(distance):
        return (head, lax.rem(device + count + GROUP * distance, count))

    def at_near(shift):
        return (head, base + lax.rem(lane + GROUP + shift, GROUP))

    sibling = (1 - head, device)
    own_rows = pl.ds(pl.multiple_of(head * half, half), half)
    other_rows = pl.ds(pl.multiple_of((1 - head) * half, half), half)

    barrier = pltpu.get_barrier_semaphore()
    partners = [at_far(d) for d in (1, 2, 3, -1, -2, -3)] + [at_near(d) for d in (1, 2, 3)] + [sibling]
    for partner in partners:
        pl.semaphore_signal(barrier, inc=1, device_id=partner, device_id_type=mesh_id)

    local = [
        pltpu.make_async_copy(w_out, w_mine.at[0], own_sem.at[0]),
        pltpu.make_async_copy(w_cross, w_mine.at[1], own_sem.at[1]),
        pltpu.make_async_copy(cross_keys.at[0], cross_mine.at[0], own_sem.at[2]),
        pltpu.make_async_copy(cross_values.at[0], cross_mine.at[1], own_sem.at[3]),
        pltpu.make_async_copy(w_query, w_query_mine, own_sem.at[4]),
        pltpu.make_async_copy(gain_self, norms.at[0], own_sem.at[5]),
        pltpu.make_async_copy(bias_self, norms.at[1], own_sem.at[6]),
        pltpu.make_async_copy(gain_cross, norms.at[2], own_sem.at[7]),
        pltpu.make_async_copy(bias_cross, norms.at[3], own_sem.at[8]),
        pltpu.make_async_copy(hidden.at[own_rows, :], hidden_mine, own_sem.at[9]),
    ]
    early = [
        pltpu.make_async_copy(queries, q_own, own_sem.at[10]),
        pltpu.make_async_copy(new_keys, k_own.at[pl.ds(0, rows), :], own_sem.at[11]),
        pltpu.make_async_copy(new_values, v_own.at[pl.ds(0, rows), :], own_sem.at[12]),
        pltpu.make_async_copy(sink_pair.at[0], k_own.at[pl.ds(rows, 16), :], own_sem.at[13]),
        pltpu.make_async_copy(sink_pair.at[1], v_own.at[pl.ds(rows, 16), :], own_sem.at[14]),
    ]
    order = [4, 1, 2, 3, 5, 6, 7, 8, 9]

    def pool_copies(s):
        return (
            pltpu.make_async_copy(pool_keys.at[0, s - 1], k_buf.at[s - 1], kv_sem.at[0, s - 1]),
            pltpu.make_async_copy(pool_values.at[0, s - 1], v_buf.at[s - 1], kv_sem.at[1, s - 1]),
        )

    for copy in early:
        copy.start()

    pad = k_own.shape[0] - rows - 16
    k_own[rows + 16 :, :] = jnp.zeros((pad, width), jnp.bfloat16)
    v_own[rows + 16 :, :] = jnp.zeros((pad, width), jnp.bfloat16)

    pl.semaphore_wait(barrier, len(partners))

    def remote(source, target, send, recv, device_id):
        return pltpu.make_async_remote_copy(
            src_ref=source,
            dst_ref=target,
            send_sem=send,
            recv_sem=recv,
            device_id=device_id,
            device_id_type=mesh_id,
        )

    def query_far(distance):
        i = distance - 1
        return remote(queries, q_far.at[i], qf_send.at[i], qf_recv.at[i], at_far(distance))

    def query_near(s, source):
        return remote(source, q_near.at[s - 1], qn_send.at[s - 1], qn_recv.at[s - 1], at_near(s % GROUP))

    def part_near(s):
        shift = lax.rem(s, GROUP)
        target = (head, base + lax.rem(lane + GROUP - shift, GROUP))
        return remote(part.at[s - 1], near.at[s - 1], pn_send.at[s - 1], pn_recv.at[s - 1], target)

    def part_far(distance, source):
        i = distance - 1
        return remote(source, far.at[i], pf_send.at[i], pf_recv.at[i], at_far(-distance))

    query_far(2).start()
    query_far(1).start()
    last = lane == GROUP - 1

    @pl.when(last)
    def _():
        query_far(3).start()

    @pl.when(jnp.logical_not(last))
    def _():
        far[2] = jnp.zeros(far.shape[1:], far.dtype)

    moves = [s for s in range(1, slots + 1) if s % GROUP]

    def forward(distance):
        source = queries if distance == 0 else q_far.at[distance - 1]
        for s in moves:
            if s // GROUP == distance or s // GROUP + 1 == distance:
                wraps = lane + s % GROUP >= GROUP
                here = wraps if s // GROUP + 1 == distance else jnp.logical_not(wraps)

                @pl.when(here)
                def _():
                    query_near(s, source).start()

    forward(0)
    for s in order:
        for copy in pool_copies(s):
            copy.start()
    for copy in local:
        copy.start()
    to_sibling = [
        (hidden.at[other_rows, :], hidden_theirs),
        (w_out, w_theirs.at[0]),
        (cross_keys.at[0], cross_theirs.at[0]),
        (cross_values.at[0], cross_theirs.at[1]),
        (w_query, w_theirs_query),
        (w_cross, w_theirs.at[1]),
    ]
    shared = [
        remote(a, b, sib_send.at[i], sib_recv.at[i], sibling) for i, (a, b) in enumerate(to_sibling)
    ]
    index = lax.broadcasted_iota(jnp.int32, (k_own.shape[0], rows), 0)
    token = lax.broadcasted_iota(jnp.int32, (k_own.shape[0], rows), 1)
    for copy in early:
        copy.wait()
    visible = (index <= token) | ((index >= rows) & (index < rows + sinks))
    bias = jnp.where(visible, 0.0, masked_score)
    store_part(own_part, *attend_pairs(q_own[...], k_own, v_own, bias))

    def compute(s, q_ref, target):
        for copy in pool_copies(s):
            copy.wait()
        asker = lax.rem(device + count - s, count)
        keys = k_buf.shape[1]
        start = block_ids[device, s - 1] * keys - cache_lengths[asker]
        relative = start + lax.broadcasted_iota(jnp.int32, (keys, rows), 0)
        token = lax.broadcasted_iota(jnp.int32, (keys, rows), 1)
        visible = (relative > token - WINDOW) & (relative < 0)
        bias = jnp.where(visible, 0.0, masked_score)
        store_part(target, *attend_pairs(q_ref[...], k_buf.at[s - 1], v_buf.at[s - 1], bias))

    def moved_step(s, carry=0):
        remote(
            queries, q_near.at[s - 1], qn_send.at[s - 1], qn_recv.at[s - 1], sibling
        ).wait_recv()
        compute(s, q_near.at[s - 1], part.at[s - 1])
        part_near(s).start()
        return carry

    def wait_near(s, condition):
        @pl.when(condition)
        def _():
            part_near(s).wait_recv()

    query_far(1).wait_recv()
    forward(1)
    compute(4, q_far.at[0], near.at[3])
    query_far(2).wait_recv()
    forward(2)
    for copy in shared:
        copy.start()
    lax.fori_loop(1, 4, moved_step, 0)

    @pl.when(last)
    def _():
        query_far(3).wait_recv()

    forward(3)
    lax.fori_loop(5, 8, moved_step, 0)
    compute(8, q_far.at[1], near.at[7])

    def merge_group(distance):
        refs, flags = [], []
        for j in range(GROUP):
            s = GROUP * distance - lane + j
            inside = s <= slots
            wait_near(s, jnp.logical_and(inside, lane != j))
            refs.append(near.at[jnp.minimum(s, slots) - 1])
            flags.append(True if distance == 1 else inside)
        store_part(merged.at[distance - 1], *merge(refs, flags))
        part_far(distance, merged.at[distance - 1]).start()

    merge_group(1)
    moved_step(9)
    merge_group(2)

    @pl.when(last)
    def _():
        part_near(9).wait_recv()
        part_far(3, near.at[8]).start()

    refs, flags = [own_part], [True]
    for s in range(1, GROUP):
        inside = lane + s < GROUP
        wait_near(s, inside)
        refs.append(near.at[s - 1])
        flags.append(inside)
    store_part(own_merged, *merge(refs, flags))
    part_far(1, merged.at[0]).wait_recv()
    part_far(2, merged.at[1]).wait_recv()

    @pl.when(last)
    def _():
        part_far(3, near.at[8]).wait_recv()

    outs, _ = merge([own_merged] + [far.at[i] for i in range(3)], [True, True, True, last])

    for i in range(2):
        cut = slice(i * half, (i + 1) * half)
        turned[i] = jnp.concatenate([o[:, cut] for o in outs], axis=0).T.astype(jnp.bfloat16)
    send_turned = remote(turned.at[1 - head], turned_theirs, sib_send.at[6], sib_recv.at[6], sibling)
    send_turned.start()

    for copy in local:
        copy.wait()
    for copy in shared:
        copy.wait()

    def project_back(rows_in, weight):
        return lax.dot_general(
            rows_in, weight, (((1,), (1,)), ((), ())), preferred_element_type=jnp.float32
        )

    def ordered(mine, theirs):
        is_first = head == 0
        return jnp.concatenate(
            [jnp.where(is_first, mine, theirs), jnp.where(is_first, theirs, mine)], axis=1
        )

    def full_norm(pre_norm, gain, bias_row):
        row_mean = jnp.mean(pre_norm, axis=-1, keepdims=True)
        centered = pre_norm - row_mean
        row_var = jnp.mean(centered * centered, axis=-1, keepdims=True)
        return centered * lax.rsqrt(row_var + norm_eps) * gain[...] + bias_row[...]

    residual = ordered(
        hidden_mine[...].astype(jnp.float32), hidden_theirs[...].astype(jnp.float32)
    )
    pre = residual + project_back(turned[head], w_mine[0])
    send_turned.wait()
    pre = pre + project_back(turned_theirs[...], w_theirs[0])
    normed = full_norm(pre, norms.at[0], norms.at[1]).astype(jnp.bfloat16)

    enc = cross_mine.shape[1]
    seen = lax.broadcasted_iota(jnp.int32, (enc, half), 0) < enc_lengths[0]
    enc_bias = jnp.where(seen, 0.0, masked_score)
    second = normed.astype(jnp.float32)
    for wq, kv, w_back in (
        (w_query_mine, cross_mine, w_mine.at[1]),
        (w_theirs_query, cross_theirs, w_theirs.at[1]),
    ):
        cross_query = jnp.dot(normed, wq[...], preferred_element_type=jnp.float32).astype(jnp.bfloat16)
        context, _ = attend_pairs(cross_query, kv.at[0], kv.at[1], enc_bias)
        context = jnp.concatenate(context, axis=0).T.astype(jnp.bfloat16)
        second = second + project_back(context, w_back[...])
    result = full_norm(second, norms.at[2], norms.at[3])
    left, right = result[:, :width], result[:, width:]
    is_first = head == 0
    out_send[...] = jnp.where(is_first, right, left).astype(jnp.bfloat16)
    send_out = remote(out_send, out_theirs, sib_send.at[7], sib_recv.at[7], sibling)
    send_out.start()
    out[own_rows, :] = jnp.where(is_first, left, right).astype(jnp.bfloat16)

    for s in moves:
        query_near(s, queries).wait_send()
        part_near(s).wait_send()
    for distance in (1, 2):
        query_far(distance).wait_send()
        part_far(distance, merged.at[distance - 1]).wait_send()

    @pl.when(last)
    def _():
        query_far(3).wait_send()
        part_far(3, near.at[8]).wait_send()

    send_out.wait()
    out[other_rows, :] = out_theirs[...]


def per_device(
    queries,
    new_keys,
    new_values,
    sink_keys,
    sink_values,
    pool_keys,
    pool_values,
    block_ids,
    cache_lengths,
    cross_keys,
    cross_values,
    enc_lengths,
    hidden,
    w_out_t,
    gain_self,
    bias_self,
    w_cross_q,
    w_cross_out_t,
    gain_cross,
    bias_cross,
):
    count = lax.axis_size("blk")
    rows, width = queries.shape
    slots, keys = pool_keys.shape[1:3]
    sinks = sink_keys.shape[1]
    enc = cross_keys.shape[1]
    full = w_out_t.shape[0]
    half = rows // 2
    packed = width + 4 * (width // HD)
    pad = ((0, 0), (0, 16 - sinks), (0, 0))
    whole = pl.BlockSpec(memory_space=pltpu.VMEM)
    smem = pl.BlockSpec(memory_space=pltpu.SMEM)
    hbm = pl.BlockSpec(memory_space=pltpu.HBM)

    def buf(*shape):
        return pltpu.VMEM(shape, jnp.bfloat16)

    dma = pltpu.SemaphoreType.DMA
    return pl.pallas_call(
        functools.partial(layer_kernel, count, slots, sinks),
        out_shape=jax.ShapeDtypeStruct((rows, width), jnp.bfloat16),
        in_specs=[smem] * 3
        + [hbm] * 16,
        out_specs=whole,
        scratch_shapes=[
            buf(slots, keys, width),
            buf(slots, keys, width),
            buf(rows + 128, width),
            buf(rows + 128, width),
            buf(rows, width),
            buf(half, width),
            buf(full, width),
            pltpu.VMEM((4, 1, full), jnp.float32),
            buf(3, rows, width),
            buf(slots, rows, width),
            buf(slots, packed, rows),
            buf(slots, packed, rows),
            buf(2, packed, rows),
            buf(3, packed, rows),
            buf(packed, rows),
            buf(packed, rows),
            buf(2, full, width),
            buf(2, full, width),
            buf(full, width),
            buf(2, enc, width),
            buf(2, enc, width),
            buf(half, width),
            buf(2, half, width),
            buf(half, width),
            buf(half, width),
            buf(half, width),
            dma((2, slots)),
            dma((15,)),
            dma((3,)),
            dma((3,)),
            dma((slots,)),
            dma((slots,)),
            dma((slots,)),
            dma((slots,)),
            dma((3,)),
            dma((3,)),
            dma((8,)),
            dma((8,)),
        ],
        compiler_params=pltpu.CompilerParams(
            collective_id=0, has_side_effects=True, vmem_limit_bytes=64 * 1024 * 1024
        ),
        cost_estimate=pl.CostEstimate(
            flops=4 * rows * keys * width * slots,
            bytes_accessed=4 * keys * width * slots,
            transcendentals=rows * keys * slots * (width // HD),
        ),
    )(
        block_ids,
        cache_lengths,
        enc_lengths,
        queries,
        new_keys,
        new_values,
        jnp.pad(jnp.concatenate([sink_keys, sink_values], axis=0), pad),
        pool_keys,
        pool_values,
        cross_keys,
        cross_values,
        hidden,
        w_out_t,
        gain_self.reshape(1, -1),
        bias_self.reshape(1, -1),
        w_cross_q,
        w_cross_out_t,
        gain_cross.reshape(1, -1),
        bias_cross.reshape(1, -1),
    )


def solution(mesh):
    placed = (
        P("blk", "head"),
        P("blk", "head"),
        P("blk", "head"),
        P("blk", None, "head"),
        P("blk", None, "head"),
        P("blk", None, None, "head"),
        P("blk", None, None, "head"),
        P(),
        P(),
        P("blk", None, "head"),
        P("blk", None, "head"),
        P("blk"),
        P("blk", "head"),
        P(None, "head"),
        P(),
        P(),
        P(None, "head"),
        P(None, "head"),
        P(),
        P(),
    )
    return jax.shard_map(
        per_device, mesh=mesh, in_specs=placed, out_specs=P("blk", "head"), check_vma=False
    )
```
